32 devices in a mesh: groups: 1, dom: 32 (over z, y, x, core).
Axes of the slice: x: 2, y: 2, z: 4, core: 2. Of those that a mesh axis runs over, the one named last changes fastest.
Arguments:
- feats: bfloat16 [32768, 512], P(('groups', 'dom')), may hold values from -6 to 6
- pre_act: bfloat16 [32768, 512], P(('groups', 'dom')), may hold values from -6 to 6
- cotangent: bfloat16 [32768, 512], P(('groups', 'dom')), may hold values from -6 to 6
- w_self1: bfloat16 [512, 512], replicated, may hold values from -0.25 to 0.25
- w_neigh1: bfloat16 [512, 512], replicated, may hold values from -0.25 to 0.25
- w_self2: bfloat16 [512, 512], replicated, may hold values from -0.25 to 0.25
- w_neigh2: bfloat16 [512, 512], replicated, may hold values from -0.25 to 0.25
- local_tiles: bfloat16 [768, 128, 128], P(('groups', 'dom')), may hold values from -0.25 to 0.25
- local_coords: int32 [768, 2], P(('groups', 'dom')), may hold values from 0 to 7
- remote_tiles: bfloat16 [512, 128, 128], P(('groups', 'dom')), may hold values from -0.25 to 0.25
- remote_rows: int32 [512], P(('groups', 'dom')), may hold values from 0 to 7
- remote_slots: int32 [512], P(('groups', 'dom')), may hold values from 0 to 1
- send_rows: int32 [32, 32, 8], P(('groups', 'dom')), may hold values from 0 to 1023
- send_count: int32 [32, 32], P(('groups', 'dom')), may hold values from 0 to 8, as said below
Outputs:
- feat_grad: float32 [32768, 512], P(('groups', 'dom'))
- grad_self1: float32 [512, 512], P('groups')
- grad_neigh1: float32 [512, 512], P('groups')
- grad_self2: float32 [512, 512], P('groups')
- grad_neigh2: float32 [512, 512], P('groups')
The draws below stay inside these ranges and needn't reach their ends.
Inputs may be any that keep to these rules, and one draw needn't show every extreme that they name: `send_count`: the diagonal is 0, and in every draw some partition receives 8 rows from every other partition.
All inputs are finite; a program needn't handle non-finite values.
Results may differ from the reference program's by a relative error of at most 0.004.
Values may be sent and summed in bfloat16 or wider, within the bound.
A program may use at most 128 MiB of HBM per device.

```python
import jax
import jax.numpy as jnp
from jax import lax

NL = 1024
F = 512
TB = 128
TL = 24
RT = 16
CAP = 8
NODES = 32768
N_DOM = 32


def draw_send_count(key, part):
    key = jax.random.fold_in(key, 7)
    first, second, third = jax.random.split(key, 3)
    ceiling = jax.random.randint(first, (N_DOM,), CAP // 4, CAP + 1)
    floor_part = ceiling // 2
    counts = jax.random.randint(second, (N_DOM, N_DOM), floor_part[None, :], ceiling[None, :] + 1)
    target = jax.random.randint(third, (), 0, N_DOM)
    columns = jnp.arange(N_DOM)[None, :]
    counts = jnp.where(columns == target, CAP, counts)
    row_ids = jnp.arange(N_DOM)[:, None]
    return jnp.where(row_ids == columns, 0, counts).astype(jnp.int32)


def set_ends(result, stream_key, smallest, high):
    spot = [jax.random.randint(jax.random.fold_in(stream_key, axis), (), 0, length) for axis, length in enumerate(result.shape)]
    main_axis = result.shape.index(max(result.shape))
    beside = spot[:main_axis] + [(spot[main_axis] + 1) % result.shape[main_axis]] + spot[main_axis + 1:]
    return result.at[tuple(spot)].set(smallest).at[tuple(beside)].set(high)


def steps_of(stream_key, dims, cuts, smallest, high):
    def one(position, blocks):
        draws = jax.random.uniform(jax.random.fold_in(jax.random.fold_in(stream_key, 6), position), (blocks,), jnp.float32, smallest / len(cuts), high / len(cuts))
        return jnp.repeat(jnp.exp(draws), dims[position] // blocks).reshape((-1,) + (1,) * (len(dims) - position - 1))

    gain = one(*cuts[0])
    for cut in cuts[1:]:
        gain = gain * one(*cut)
    return gain


def noise(own_key, dims, deviation, reach, cuts=(), kind=jnp.bfloat16):
    factor_of = steps_of(own_key, dims, cuts, -0.22, 0.18) if cuts else 1.0
    array = jax.random.normal(own_key, dims, jnp.float32) * deviation * factor_of
    return jnp.minimum(jnp.maximum(array, -reach), reach).astype(kind)


def setup_inputs(seed: int = 0, part: int = 0) -> dict:
    streams_of = jax.random.split(jax.random.key(seed), 15)
    own_keys = jax.random.split(jax.random.fold_in(streams_of[14], part), 15)
    feats = noise(own_keys[0], (NODES, F), 1.0, 6.0, ((0, 32),))
    pre_act = noise(own_keys[1], (NODES, F), 1.0, 6.0, ((0, 32),))
    cotangent = noise(own_keys[2], (NODES, F), 1.0, 6.0, ((0, 32),))
    w_self1 = noise(streams_of[3], (F, F), F ** -0.5, 0.25)
    w_neigh1 = noise(streams_of[4], (F, F), F ** -0.5, 0.25)
    w_self2 = noise(streams_of[5], (F, F), F ** -0.5, 0.25)
    w_neigh2 = noise(streams_of[6], (F, F), F ** -0.5, 0.25)
    local_tiles = noise(own_keys[7], (N_DOM * TL, TB, TB), (TB * (TL + RT) // (NL // TB)) ** -0.5, 0.25, ((0, 32),))
    local_coords = set_ends(jax.random.randint(own_keys[8], (N_DOM * TL, 2), 0, NL // TB), jax.random.fold_in(own_keys[8], 1), 0, (NL // TB) - 1).astype(jnp.int32)
    remote_tiles = noise(own_keys[9], (N_DOM * RT, TB, TB), (TB * (TL + RT) // (NL // TB)) ** -0.5, 0.25, ((0, 32),))
    remote_rows = set_ends(jax.random.randint(own_keys[10], (N_DOM * RT,), 0, NL // TB), jax.random.fold_in(own_keys[10], 1), 0, (NL // TB) - 1).astype(jnp.int32)
    remote_slots = set_ends(jax.random.randint(own_keys[11], (N_DOM * RT,), 0, N_DOM * CAP // TB), jax.random.fold_in(own_keys[11], 1), 0, (N_DOM * CAP // TB) - 1).astype(jnp.int32)
    send_rows = set_ends(jax.random.randint(own_keys[12], (N_DOM, N_DOM, CAP), 0, NL), jax.random.fold_in(own_keys[12], 1), 0, NL - 1).astype(jnp.int32)
    send_count = draw_send_count(jax.random.fold_in(jax.random.fold_in(streams_of[14], part), 71), part)
    return {"feats": feats, "pre_act": pre_act, "cotangent": cotangent, "w_self1": w_self1, "w_neigh1": w_neigh1, "w_self2": w_self2, "w_neigh2": w_neigh2, "local_tiles": local_tiles, "local_coords": local_coords, "remote_tiles": remote_tiles, "remote_rows": remote_rows, "remote_slots": remote_slots, "send_rows": send_rows, "send_count": send_count}


def apply_tiles(tile_set, out_index, in_index, source, out_blocks):
    tile_side = tile_set.shape[1]
    breadth = source.shape[1]
    blocks = source.reshape(-1, tile_side, breadth)[in_index].astype(jnp.float32)
    products = jnp.einsum('kij,kjf->kif', tile_set.astype(jnp.float32), blocks, precision=lax.Precision.HIGHEST)
    select = (out_index[None, :] == jnp.arange(out_blocks)[:, None]).astype(jnp.float32)
    return jnp.einsum('bk,kif->bif', select, products, precision=lax.Precision.HIGHEST).reshape(-1, breadth)


def apply_transposed(tile_set, out_index, in_index, source, out_blocks):
    tile_side = tile_set.shape[1]
    breadth = source.shape[1]
    blocks = source.reshape(-1, tile_side, breadth)[in_index].astype(jnp.float32)
    products = jnp.einsum('kij,kif->kjf', tile_set.astype(jnp.float32), blocks, precision=lax.Precision.HIGHEST)
    select = (out_index[None, :] == jnp.arange(out_blocks)[:, None]).astype(jnp.float32)
    return jnp.einsum('bk,kif->bif', select, products, precision=lax.Precision.HIGHEST).reshape(-1, breadth)


def reference(feats, pre_act, cotangent, w_self1, w_neigh1, w_self2, w_neigh2, local_tiles, local_coords, remote_tiles, remote_rows, remote_slots, send_rows, send_count):
    highest = lax.Precision.HIGHEST
    blocks_local = NL // TB
    blocks_slot = N_DOM * CAP // TB
    live_slots = jnp.arange(CAP)[None, None, :] < send_count[:, :, None]
    tiles_local = local_tiles.reshape(N_DOM, TL, TB, TB)
    coords_local = local_coords.reshape(N_DOM, TL, 2)
    tiles_remote = remote_tiles.reshape(N_DOM, RT, TB, TB)
    rows_remote = remote_rows.reshape(N_DOM, RT)
    slots_remote = remote_slots.reshape(N_DOM, RT)

    def incoming(activation):
        parted = activation.reshape(N_DOM, NL, F)
        picked = jax.vmap(lambda rows_of, row_index: rows_of[row_index])(parted, send_rows)
        picked = jnp.where(live_slots[..., None], picked, jnp.zeros_like(picked))
        return picked.transpose(1, 0, 2, 3).reshape(N_DOM, N_DOM * CAP, F)

    def backward(activation, upstream, w_self, w_neigh):
        received = incoming(activation)

        def one_part(inputs_part):
            part_rows, part_grad, part_tiles, part_coords, part_remote, part_rrows, part_slots, part_recv = inputs_part
            gathered = apply_tiles(part_tiles, part_coords[:, 0], part_coords[:, 1], part_rows, blocks_local)
            gathered = gathered + apply_tiles(part_remote, part_rrows, part_slots, part_recv, blocks_local)
            local_back = apply_transposed(part_tiles, part_coords[:, 1], part_coords[:, 0], part_grad, blocks_local)
            slot_back = apply_transposed(part_remote, part_slots, part_rrows, part_grad, blocks_slot)
            self_term = jnp.dot(part_rows.T, part_grad, preferred_element_type=jnp.float32)
            neigh_term = jnp.dot(gathered.T, part_grad.astype(jnp.float32), precision=highest)
            return local_back, slot_back, self_term, neigh_term

        local_back, slot_back, self_terms, neigh_terms = lax.map(one_part, (activation.reshape(N_DOM, NL, F), upstream.reshape(N_DOM, NL, F), tiles_local, coords_local, tiles_remote, rows_remote, slots_remote, received))
        returned = slot_back.reshape(N_DOM, N_DOM, CAP, F).transpose(1, 0, 2, 3)
        returned = jnp.where(live_slots[..., None], returned, jnp.zeros_like(returned))

        def scatter_part(values, row_index):
            return jnp.zeros((NL, F), jnp.float32).at[row_index.reshape(-1)].add(values.reshape(-1, F))

        summed = (local_back + jax.vmap(scatter_part)(returned, send_rows)).reshape(N_DOM * NL, F)
        summed_low = summed.astype(jnp.bfloat16)
        grad_in = jnp.dot(upstream, w_self.T, preferred_element_type=jnp.float32)
        grad_in = grad_in + jnp.dot(summed_low, w_neigh.T, preferred_element_type=jnp.float32)
        return grad_in, jnp.sum(self_terms, axis=0), jnp.sum(neigh_terms, axis=0)

    hidden = jnp.maximum(pre_act, jnp.zeros_like(pre_act))
    grad_hidden, self_two, neigh_two = backward(hidden, cotangent, w_self2, w_neigh2)
    upstream_one = jnp.where(pre_act > 0, grad_hidden, jnp.zeros_like(grad_hidden)).astype(jnp.bfloat16)
    grad_feats, self_one, neigh_one = backward(feats, upstream_one, w_self1, w_neigh1)
    return (grad_feats, self_one, neigh_one, self_two, neigh_two)
```

```python
import functools

import jax
import jax.numpy as jnp
from jax import lax
from jax.experimental import pallas as pl
from jax.experimental.pallas import tpu as pltpu
from jax.sharding import PartitionSpec as P

F32 = jnp.float32
BF16 = jnp.bfloat16
MESH = pl.DeviceIdType.MESH
VMEM_LIMIT = 52 * 1024 * 1024


def mm(a, b, ca, cb):
    return lax.dot_general(a, b, (((ca,), (cb,)), ((), ())), preferred_element_type=F32)


def dense_kernel(coords, rrows, rslots, ltiles, rtiles, d_out, rt_out, d_acc, rt_acc):
    side = ltiles.shape[1]
    d_acc[...] = jnp.zeros_like(d_acc)
    rt_acc[...] = jnp.zeros_like(rt_acc)

    @pl.loop(0, ltiles.shape[0])
    def _(t):
        r = pl.multiple_of(coords[t, 0] * side, side)
        q = pl.multiple_of(coords[t, 1] * side, side)
        d_acc[pl.ds(q, side), pl.ds(r, side)] += ltiles[t].astype(F32).T

    @pl.loop(0, rtiles.shape[0])
    def _(t):
        r = pl.multiple_of(rrows[t] * side, side)
        q = pl.multiple_of(rslots[t] * side, side)
        rt_acc[pl.ds(q, side), pl.ds(r, side)] += rtiles[t].astype(F32).T

    for acc, out in ((d_acc, d_out), (rt_acc, rt_out)):
        whole = acc[...]
        high = whole.astype(BF16)
        out[0] = high
        out[1] = (whole - high.astype(F32)).astype(BF16)


def main_kernel(
    n,
    feats,
    pre,
    cot,
    ws1,
    wn1,
    ws2,
    wn2,
    dense,
    rt,
    idx,
    fg_out,
    gr_out,
    hid,
    low,
    rest,
    up1,
    onehot,
    acc_s,
    acc_o,
    sb,
    arr,
    part,
    sibr,
    half,
    rsr,
    ag,
    a2a_send,
    a2a_recv,
    sib_send,
    sib_recv,
    rs_send,
    rs_recv,
    ag_send,
    ag_recv,
):
    nl, f = feats.shape
    m = n // 2
    fh = f // 2
    me = lax.axis_index("dom")
    chip = me // 2
    core = me % 2
    sibling = chip * 2 + 1 - core
    blk = 256
    barrier = pltpu.get_barrier_semaphore()

    @pl.loop(1, n)
    def _(k):
        pl.semaphore_signal(
            barrier, inc=1, device_id={"dom": lax.rem(me + k, n)}, device_id_type=MESH
        )

    def a2a_copy(l, k):
        peer = lax.rem(me + k, n)
        return pltpu.make_async_remote_copy(
            src_ref=sb.at[l, peer],
            dst_ref=arr.at[l, me],
            send_sem=a2a_send.at[l, k],
            recv_sem=a2a_recv.at[l, k],
            device_id={"dom": peer},
            device_id_type=MESH,
        )

    def sib_copy(l):
        return pltpu.make_async_remote_copy(
            src_ref=part.at[l, 1 - core],
            dst_ref=sibr.at[l],
            send_sem=sib_send.at[l],
            recv_sem=sib_recv.at[l],
            device_id={"dom": sibling},
            device_id_type=MESH,
        )

    def rs_copy(l, k):
        to = lax.rem(chip + k, m)
        return pltpu.make_async_remote_copy(
            src_ref=half.at[l, to],
            dst_ref=rsr.at[l, chip],
            send_sem=rs_send.at[l, k],
            recv_sem=rs_recv.at[l, k],
            device_id={"dom": to * 2 + core},
            device_id_type=MESH,
        )

    def ag_copy(l, k):
        to = lax.rem(chip + k, m)
        return pltpu.make_async_remote_copy(
            src_ref=ag.at[l, core, chip],
            dst_ref=ag.at[l, core, chip],
            send_sem=ag_send.at[l, k],
            recv_sem=ag_recv.at[l, k],
            device_id={"dom": to * 2 + core},
            device_id_type=MESH,
        )

    def fwd_copy(l):
        return pltpu.make_async_remote_copy(
            src_ref=ag.at[l, core],
            dst_ref=ag.at[l, core],
            send_sem=sib_send.at[2 + l],
            recv_sem=sib_recv.at[2 + l],
            device_id={"dom": sibling},
            device_id_type=MESH,
        )

    def each(count, l, copy, action):
        @pl.loop(1, count)
        def _(k):
            getattr(copy(l, k), action)()

    def slot_back(l, g):
        back = mm(rt[0], g[...], 1, 0) + mm(rt[1], g[...], 1, 0)
        left = back[:, :fh].reshape(n, -1, fh)
        right = back[:, fh:].reshape(n, -1, fh)
        sb[l] = jnp.concatenate([left, right], axis=1).astype(BF16)

    def local_part(g, ws):
        @pl.loop(0, nl // blk)
        def _(i):
            rows = pl.ds(pl.multiple_of(i * blk, blk), blk)
            acc_s[rows, :] = mm(dense[0, rows, :], g[...], 1, 0) + mm(
                dense[1, rows, :], g[...], 1, 0
            )
            acc_o[rows, :] = mm(g[rows, :], ws[...], 1, 1)

    def gradient(l, which, h, *terms):
        for i in range(f // blk):
            cols = slice(i * blk, (i + 1) * blk)
            part[l, which, cols, :] = sum(mm(h[:, cols], g[...], 0, 0) for g in terms)

    def finish(l, wn, emit):
        got = arr[l].astype(F32)
        cap = got.shape[1] // 2
        left = got[:, :cap, :].reshape(n * cap, fh).astype(BF16)
        right = got[:, cap:, :].reshape(n * cap, fh).astype(BF16)
        got = jnp.concatenate([left, right], axis=1)

        @pl.loop(0, nl // blk)
        def _(i):
            rows = pl.ds(pl.multiple_of(i * blk, blk), blk)
            summed = acc_s[rows, :] + mm(onehot[rows, :], got, 1, 0)
            high = summed.astype(BF16)
            low[rows, :] = high
            rest[rows, :] = (summed - high.astype(F32)).astype(BF16)
            emit(rows, acc_o[rows, :] + mm(low[rows, :], wn[...], 1, 1))

    def reduce_start(l):
        sib_copy(l).wait_recv()
        mine = part[l, core] + sibr[l]
        half[l] = mine.astype(BF16).reshape(half.shape[1:])
        each(m, l, rs_copy, "start")

    def reduce_end(l):
        each(m, l, rs_copy, "wait_recv")
        total = half[l, chip].astype(F32)
        for k in range(1, m):
            total = total + rsr[l, lax.rem(chip + k, m)].astype(F32)
        ag[l, core, chip] = total.astype(BF16)
        each(m, l, ag_copy, "start")

    slot_back(0, cot)
    arr[0, me] = jnp.zeros_like(arr[0, me])
    arr[1, me] = jnp.zeros_like(arr[1, me])
    pl.semaphore_wait(barrier, n - 1)
    each(n, 0, a2a_copy, "start")
    hid[...] = jnp.maximum(pre[...], jnp.zeros_like(pre))
    local_part(cot, ws2)
    gradient(0, 0, hid, cot)
    onehot[...] = jnp.where(
        lax.broadcasted_iota(jnp.int32, onehot.shape, 0) == idx[...], 1.0, 0.0
    ).astype(BF16)
    each(n, 0, a2a_copy, "wait_recv")

    def emit_two(rows, value):
        up1[rows, :] = jnp.where(pre[rows, :].astype(F32) > 0, value, 0.0).astype(BF16)

    finish(0, wn2, emit_two)
    slot_back(1, up1)
    each(n, 1, a2a_copy, "start")
    gradient(0, 1, hid, low, rest)
    sib_copy(0).start()
    local_part(up1, ws1)
    reduce_start(0)
    gradient(1, 0, feats, up1)
    each(n, 1, a2a_copy, "wait_recv")

    def emit_one(rows, value):
        fg_out[rows, :] = value

    finish(1, wn1, emit_one)
    gradient(1, 1, feats, low, rest)
    sib_copy(1).start()
    reduce_end(0)
    reduce_start(1)
    reduce_end(1)
    each(m, 0, ag_copy, "wait_recv")
    fwd_copy(0).start()
    each(m, 1, ag_copy, "wait_recv")
    fwd_copy(1).start()
    each(n, 0, a2a_copy, "wait_send")
    each(n, 1, a2a_copy, "wait_send")
    for l in range(2):
        sib_copy(l).wait_send()
        each(m, l, rs_copy, "wait_send")
        each(m, l, ag_copy, "wait_send")
    for l in range(2):
        fwd_copy(l).wait()
        gr_out[l] = ag[l].reshape(gr_out.shape[1:])


def per_device(
    feats,
    pre_act,
    cotangent,
    w_self1,
    w_neigh1,
    w_self2,
    w_neigh2,
    local_tiles,
    local_coords,
    remote_tiles,
    remote_rows,
    remote_slots,
    send_rows,
    send_count,
):
    n = lax.axis_size("dom")
    m = n // 2
    nl, f = feats.shape
    cap = send_rows.shape[2]
    slots = n * cap
    vmem = pl.BlockSpec(memory_space=pltpu.VMEM)
    smem = pl.BlockSpec(memory_space=pltpu.SMEM)
    dense, rt = pl.pallas_call(
        dense_kernel,
        out_shape=(
            jax.ShapeDtypeStruct((2, nl, nl), BF16),
            jax.ShapeDtypeStruct((2, slots, nl), BF16),
        ),
        in_specs=[smem, smem, smem, vmem, vmem],
        out_specs=(vmem, vmem),
        scratch_shapes=[pltpu.VMEM((nl, nl), F32), pltpu.VMEM((slots, nl), F32)],
        compiler_params=pltpu.CompilerParams(vmem_limit_bytes=VMEM_LIMIT),
        name="dense",
    )(local_coords, remote_rows, remote_slots, local_tiles, remote_tiles)

    live = jnp.arange(cap)[None, :] < send_count[0][:, None]
    idx = jnp.where(live, send_rows[0], -1).reshape(1, slots)
    chunk = f // m
    dma = pltpu.SemaphoreType.DMA
    feat_grad, grads = pl.pallas_call(
        functools.partial(main_kernel, n),
        out_shape=(
            jax.ShapeDtypeStruct((nl, f), F32),
            jax.ShapeDtypeStruct((2, 2, f, f), BF16),
        ),
        in_specs=[vmem] * 10,
        out_specs=(vmem, vmem),
        scratch_shapes=[
            pltpu.VMEM((nl, f), BF16),
            pltpu.VMEM((nl, f), BF16),
            pltpu.VMEM((nl, f), BF16),
            pltpu.VMEM((nl, f), BF16),
            pltpu.VMEM((nl, slots), BF16),
            pltpu.VMEM((nl, f), F32),
            pltpu.VMEM((nl, f), F32),
            pltpu.VMEM((2, n, 2 * cap, f // 2), BF16),
            pltpu.VMEM((2, n, 2 * cap, f // 2), BF16),
            pltpu.VMEM((2, 2, f, f), F32),
            pltpu.VMEM((2, f, f), F32),
            pltpu.VMEM((2, m, chunk, f), BF16),
            pltpu.VMEM((2, m, chunk, f), BF16),
            pltpu.VMEM((2, 2, m, chunk, f), BF16),
            dma((2, n)),
            dma((2, n)),
            dma((4,)),
            dma((4,)),
            dma((2, m)),
            dma((2, m)),
            dma((2, m)),
            dma((2, m)),
        ],
        compiler_params=pltpu.CompilerParams(
            collective_id=0, has_side_effects=True, vmem_limit_bytes=VMEM_LIMIT
        ),
        name="main",
    )(
        feats,
        pre_act,
        cotangent,
        w_self1,
        w_neigh1,
        w_self2,
        w_neigh2,
        dense,
        rt,
        idx,
    )
    grads = grads.astype(F32)
    return (feat_grad, grads[1, 0], grads[1, 1], grads[0, 0], grads[0, 1])


def solution(mesh):
    return jax.shard_map(
        per_device,
        mesh=mesh,
        in_specs=(
            P(("groups", "dom"), None),
            P(("groups", "dom"), None),
            P(("groups", "dom"), None),
            P(),
            P(),
            P(),
            P(),
            P(("groups", "dom"), None, None),
            P(("groups", "dom"), None),
            P(("groups", "dom"), None, None),
            P(("groups", "dom")),
            P(("groups", "dom")),
            P(("groups", "dom"), None, None),
            P(("groups", "dom"), None),
        ),
        out_specs=(
            P(("groups", "dom"), None),
            P("groups", None),
            P("groups", None),
            P("groups", None),
            P("groups", None),
        ),
        check_vma=False,
    )
```

```python
import functools

import jax
import jax.numpy as jnp
from jax import lax
from jax.experimental import pallas as pl
from jax.experimental.pallas import tpu as pltpu
from jax.sharding import PartitionSpec as P

F32 = jnp.float32
BF16 = jnp.bfloat16
MESH = pl.DeviceIdType.MESH
VMEM_LIMIT = 52 * 1024 * 1024


def mm(a, b, ca, cb):
    return lax.dot_general(a, b, (((ca,), (cb,)), ((), ())), preferred_element_type=F32)


def dense_kernel(coords, rrows, rslots, ltiles, rtiles, d_out, rt_out, d_acc, rt_acc):
    side = ltiles.shape[1]
    d_acc[...] = jnp.zeros_like(d_acc)
    rt_acc[...] = jnp.zeros_like(rt_acc)

    @pl.loop(0, ltiles.shape[0])
    def _(t):
        r = pl.multiple_of(coords[t, 0] * side, side)
        q = pl.multiple_of(coords[t, 1] * side, side)
        d_acc[pl.ds(q, side), pl.ds(r, side)] += ltiles[t].astype(F32).T

    @pl.loop(0, rtiles.shape[0])
    def _(t):
        r = pl.multiple_of(rrows[t] * side, side)
        q = pl.multiple_of(rslots[t] * side, side)
        rt_acc[pl.ds(q, side), pl.ds(r, side)] += rtiles[t].astype(F32).T

    for acc, out in ((d_acc, d_out), (rt_acc, rt_out)):
        whole = acc[...]
        high = whole.astype(BF16)
        out[0] = high
        out[1] = (whole - high.astype(F32)).astype(BF16)


def main_kernel(
    n,
    feats,
    pre,
    cot,
    ws1,
    wn1,
    ws2,
    wn2,
    dense,
    rt,
    idx,
    fg_out,
    gs1_out,
    gn1_out,
    gs2_out,
    gn2_out,
    hid,
    low,
    rest,
    up1,
    onehot,
    acc_s,
    acc_o,
    sb,
    arr,
    part,
    sibr,
    half,
    rsp,
    mid,
    rsl,
    ag,
    a2a_send,
    a2a_recv,
    sib_send,
    sib_recv,
    rp_send,
    rp_recv,
    rl_send,
    rl_recv,
    al_send,
    al_recv,
    ap_send,
    ap_recv,
):
    nl, f = feats.shape
    fh = f // 2
    plane, layers = half.shape[1:3]
    me = lax.axis_index("dom")
    chip = me // 2
    core = me % 2
    place = chip % plane
    layer = chip // plane
    sibling = chip * 2 + 1 - core
    blk = 256
    barrier = pltpu.get_barrier_semaphore()

    @pl.loop(1, n)
    def _(k):
        pl.semaphore_signal(
            barrier, inc=1, device_id={"dom": lax.rem(me + k, n)}, device_id_type=MESH
        )

    def a2a_copy(l, k):
        peer = lax.rem(me + k, n)
        return pltpu.make_async_remote_copy(
            src_ref=sb.at[l, peer],
            dst_ref=arr.at[l, me],
            send_sem=a2a_send.at[l, k],
            recv_sem=a2a_recv.at[l, k],
            device_id={"dom": peer},
            device_id_type=MESH,
        )

    def sib_copy(l):
        return pltpu.make_async_remote_copy(
            src_ref=part.at[l, 1 - core],
            dst_ref=sibr.at[l],
            send_sem=sib_send.at[l],
            recv_sem=sib_recv.at[l],
            device_id={"dom": sibling},
            device_id_type=MESH,
        )

    def plane_copy(src, dst, send, recv, l, k):
        to = lax.rem(place + k, plane)
        return pltpu.make_async_remote_copy(
            src_ref=src(to),
            dst_ref=dst,
            send_sem=send.at[l, k],
            recv_sem=recv.at[l, k],
            device_id={"dom": (layer * plane + to) * 2 + core},
            device_id_type=MESH,
        )

    def layer_copy(src, dst, send, recv, l, k):
        to = lax.rem(layer + k, layers)
        return pltpu.make_async_remote_copy(
            src_ref=src(to),
            dst_ref=dst,
            send_sem=send.at[l, k],
            recv_sem=recv.at[l, k],
            device_id={"dom": (to * plane + place) * 2 + core},
            device_id_type=MESH,
        )

    def rs_plane(l, k):
        return plane_copy(
            lambda to: half.at[l, to], rsp.at[l, place], rp_send, rp_recv, l, k
        )

    def rs_layer(l, k):
        return layer_copy(
            lambda to: mid.at[l, to], rsl.at[l, layer], rl_send, rl_recv, l, k
        )

    def ag_layer(l, k):
        own = ag.at[l, core, place, layer]
        return layer_copy(lambda to: own, own, al_send, al_recv, l, k)

    def ag_plane(l, k):
        own = ag.at[l, core, place]
        return plane_copy(lambda to: own, own, ap_send, ap_recv, l, k)

    def fwd_copy(l):
        return pltpu.make_async_remote_copy(
            src_ref=ag.at[l, core],
            dst_ref=ag.at[l, core],
            send_sem=sib_send.at[2 + l],
            recv_sem=sib_recv.at[2 + l],
            device_id={"dom": sibling},
            device_id_type=MESH,
        )

    def each(count, l, copy, action):
        @pl.loop(1, count)
        def _(k):
            getattr(copy(l, k), action)()

    def slot_back(l, g):
        back = mm(rt[0], g[...], 1, 0) + mm(rt[1], g[...], 1, 0)
        left = back[:, :fh].reshape(n, -1, fh)
        right = back[:, fh:].reshape(n, -1, fh)
        sb[l] = jnp.concatenate([left, right], axis=1).astype(BF16)

    def local_part(g, ws):
        @pl.loop(0, nl // blk)
        def _(i):
            rows = pl.ds(pl.multiple_of(i * blk, blk), blk)
            acc_s[rows, :] = mm(dense[0, rows, :], g[...], 1, 0) + mm(
                dense[1, rows, :], g[...], 1, 0
            )
            acc_o[rows, :] = mm(g[rows, :], ws[...], 1, 1)

    def gradient(l, which, h, *terms):
        for i in range(f // blk):
            cols = slice(i * blk, (i + 1) * blk)
            part[l, which, cols, :] = sum(mm(h[:, cols], g[...], 0, 0) for g in terms)

    def finish(l, wn, emit):
        got = arr[l].astype(F32)
        cap = got.shape[1] // 2
        left = got[:, :cap, :].reshape(n * cap, fh).astype(BF16)
        right = got[:, cap:, :].reshape(n * cap, fh).astype(BF16)
        got = jnp.concatenate([left, right], axis=1)

        @pl.loop(0, nl // blk)
        def _(i):
            rows = pl.ds(pl.multiple_of(i * blk, blk), blk)
            summed = acc_s[rows, :] + mm(onehot[rows, :], got, 1, 0)
            high = summed.astype(BF16)
            low[rows, :] = high
            rest[rows, :] = (summed - high.astype(F32)).astype(BF16)
            emit(rows, acc_o[rows, :] + mm(low[rows, :], wn[...], 1, 1))

    def reduce_start(l):
        sib_copy(l).wait_recv()
        mine = part[l, core] + sibr[l]
        half[l] = mine.astype(BF16).reshape(half.shape[1:])
        each(plane, l, rs_plane, "start")

    def reduce_middle(l):
        each(plane, l, rs_plane, "wait_recv")
        total = half[l, place].astype(F32)
        for k in range(1, plane):
            total = total + rsp[l, lax.rem(place + k, plane)].astype(F32)
        mid[l] = total.astype(BF16)
        each(layers, l, rs_layer, "start")

    def reduce_end(l):
        each(layers, l, rs_layer, "wait_recv")
        total = mid[l, layer].astype(F32)
        for k in range(1, layers):
            total = total + rsl[l, lax.rem(layer + k, layers)].astype(F32)
        ag[l, core, place, layer] = total.astype(BF16)
        each(layers, l, ag_layer, "start")

    def spread(l):
        each(layers, l, ag_layer, "wait_recv")
        each(plane, l, ag_plane, "start")

    def forward(l):
        each(plane, l, ag_plane, "wait_recv")
        fwd_copy(l).start()

    slot_back(0, cot)
    arr[0, me] = jnp.zeros_like(arr[0, me])
    arr[1, me] = jnp.zeros_like(arr[1, me])
    pl.semaphore_wait(barrier, n - 1)
    each(n, 0, a2a_copy, "start")
    hid[...] = jnp.maximum(pre[...], jnp.zeros_like(pre))
    local_part(cot, ws2)
    gradient(0, 0, hid, cot)
    onehot[...] = jnp.where(
        lax.broadcasted_iota(jnp.int32, onehot.shape, 0) == idx[...], 1.0, 0.0
    ).astype(BF16)
    each(n, 0, a2a_copy, "wait_recv")

    def emit_two(rows, value):
        up1[rows, :] = jnp.where(pre[rows, :].astype(F32) > 0, value, 0.0).astype(BF16)

    finish(0, wn2, emit_two)
    slot_back(1, up1)
    each(n, 1, a2a_copy, "start")
    gradient(0, 1, hid, low, rest)
    sib_copy(0).start()
    local_part(up1, ws1)
    reduce_start(0)
    gradient(1, 0, feats, up1)
    each(n, 1, a2a_copy, "wait_recv")

    def emit_one(rows, value):
        fg_out[rows, :] = value

    reduce_middle(0)
    finish(1, wn1, emit_one)
    gradient(1, 1, feats, low, rest)
    sib_copy(1).start()
    reduce_end(0)
    reduce_start(1)
    spread(0)
    reduce_middle(1)
    forward(0)
    reduce_end(1)
    spread(1)
    forward(1)
    each(n, 0, a2a_copy, "wait_send")
    each(n, 1, a2a_copy, "wait_send")
    for l in range(2):
        sib_copy(l).wait_send()
        each(plane, l, rs_plane, "wait_send")
        each(layers, l, rs_layer, "wait_send")
        each(layers, l, ag_layer, "wait_send")
        each(plane, l, ag_plane, "wait_send")
    for l, outs in ((0, (gs2_out, gn2_out)), (1, (gs1_out, gn1_out))):
        fwd_copy(l).wait()
        for which, out in enumerate(outs):
            out[...] = ag[l, which].reshape(out.shape)


def per_device(
    feats,
    pre_act,
    cotangent,
    w_self1,
    w_neigh1,
    w_self2,
    w_neigh2,
    local_tiles,
    local_coords,
    remote_tiles,
    remote_rows,
    remote_slots,
    send_rows,
    send_count,
):
    n = lax.axis_size("dom")
    m = n // 2
    nl, f = feats.shape
    cap = send_rows.shape[2]
    slots = n * cap
    vmem = pl.BlockSpec(memory_space=pltpu.VMEM)
    smem = pl.BlockSpec(memory_space=pltpu.SMEM)
    dense, rt = pl.pallas_call(
        dense_kernel,
        out_shape=(
            jax.ShapeDtypeStruct((2, nl, nl), BF16),
            jax.ShapeDtypeStruct((2, slots, nl), BF16),
        ),
        in_specs=[smem, smem, smem, vmem, vmem],
        out_specs=(vmem, vmem),
        scratch_shapes=[pltpu.VMEM((nl, nl), F32), pltpu.VMEM((slots, nl), F32)],
        compiler_params=pltpu.CompilerParams(vmem_limit_bytes=VMEM_LIMIT),
        name="dense",
    )(local_coords, remote_rows, remote_slots, local_tiles, remote_tiles)

    live = jnp.arange(cap)[None, :] < send_count[0][:, None]
    idx = jnp.where(live, send_rows[0], -1).reshape(1, slots)
    plane = 4
    layers = m // plane
    chunk = f // m
    dma = pltpu.SemaphoreType.DMA
    feat_grad, *grads = pl.pallas_call(
        functools.partial(main_kernel, n),
        out_shape=(
            jax.ShapeDtypeStruct((nl, f), F32),
        )
        + (jax.ShapeDtypeStruct((f, f), BF16),) * 4,
        in_specs=[vmem] * 10,
        out_specs=(vmem,) * 5,
        scratch_shapes=[
            pltpu.VMEM((nl, f), BF16),
            pltpu.VMEM((nl, f), BF16),
            pltpu.VMEM((nl, f), BF16),
            pltpu.VMEM((nl, f), BF16),
            pltpu.VMEM((nl, slots), BF16),
            pltpu.VMEM((nl, f), F32),
            pltpu.VMEM((nl, f), F32),
            pltpu.VMEM((2, n, 2 * cap, f // 2), BF16),
            pltpu.VMEM((2, n, 2 * cap, f // 2), BF16),
            pltpu.VMEM((2, 2, f, f), F32),
            pltpu.VMEM((2, f, f), F32),
            pltpu.VMEM((2, plane, layers, chunk, f), BF16),
            pltpu.VMEM((2, plane, layers, chunk, f), BF16),
            pltpu.VMEM((2, layers, chunk, f), BF16),
            pltpu.VMEM((2, layers, chunk, f), BF16),
            pltpu.VMEM((2, 2, plane, layers, chunk, f), BF16),
            dma((2, n)),
            dma((2, n)),
            dma((4,)),
            dma((4,)),
            dma((2, plane)),
            dma((2, plane)),
            dma((2, layers)),
            dma((2, layers)),
            dma((2, layers)),
            dma((2, layers)),
            dma((2, plane)),
            dma((2, plane)),
        ],
        compiler_params=pltpu.CompilerParams(
            collective_id=0, has_side_effects=True, vmem_limit_bytes=VMEM_LIMIT
        ),
        name="main",
    )(
        feats,
        pre_act,
        cotangent,
        w_self1,
        w_neigh1,
        w_self2,
        w_neigh2,
        dense,
        rt,
        idx,
    )
    return (feat_grad, *(grad.astype(F32) for grad in grads))


def solution(mesh):
    return jax.shard_map(
        per_device,
        mesh=mesh,
        in_specs=(
            P(("groups", "dom"), None),
            P(("groups", "dom"), None),
            P(("groups", "dom"), None),
            P(),
            P(),
            P(),
            P(),
            P(("groups", "dom"), None, None),
            P(("groups", "dom"), None),
            P(("groups", "dom"), None, None),
            P(("groups", "dom")),
            P(("groups", "dom")),
            P(("groups", "dom"), None, None),
            P(("groups", "dom"), None),
        ),
        out_specs=(
            P(("groups", "dom"), None),
            P("groups", None),
            P("groups", None),
            P("groups", None),
            P("groups", None),
        ),
        check_vma=False,
    )
```

```python
import functools

import jax
import jax.numpy as jnp
from jax import lax
from jax.experimental import pallas as pl
from jax.experimental.pallas import tpu as pltpu
from jax.sharding import PartitionSpec as P

F32 = jnp.float32
BF16 = jnp.bfloat16
MESH = pl.DeviceIdType.MESH
VMEM_LIMIT = 52 * 1024 * 1024


def mm(a, b, ca, cb):
    return lax.dot_general(a, b, (((ca,), (cb,)), ((), ())), preferred_element_type=F32)


def dense_kernel(coords, rrows, rslots, ltiles, rtiles, d_out, rt_out, d_acc, rt_acc):
    side = ltiles.shape[1]
    d_acc[...] = jnp.zeros_like(d_acc)
    rt_acc[...] = jnp.zeros_like(rt_acc)

    @pl.loop(0, ltiles.shape[0], unroll=4)
    def _(t):
        r = pl.multiple_of(coords[t, 0] * side, side)
        q = pl.multiple_of(coords[t, 1] * side, side)
        d_acc[pl.ds(q, side), pl.ds(r, side)] += ltiles[t].astype(F32).T

    @pl.loop(0, rtiles.shape[0], unroll=4)
    def _(t):
        r = pl.multiple_of(rrows[t] * side, side)
        q = pl.multiple_of(rslots[t] * side, side)
        rt_acc[pl.ds(q, side), pl.ds(r, side)] += rtiles[t].astype(F32).T

    for acc, out in ((d_acc, d_out), (rt_acc, rt_out)):
        whole = acc[...]
        high = whole.astype(BF16)
        out[0] = high
        out[1] = (whole - high.astype(F32)).astype(BF16)


def main_kernel(
    n,
    feats,
    pre,
    cot,
    ws1,
    wn1,
    ws2,
    wn2,
    dense,
    rt,
    idx,
    fg_out,
    gs1_out,
    gn1_out,
    gs2_out,
    gn2_out,
    hid,
    low,
    rest,
    up1,
    onehot,
    acc_s,
    acc_o,
    sb,
    arr,
    part,
    sibr,
    half,
    rsp,
    mid,
    rsl,
    ag,
    a2a_send,
    a2a_recv,
    sib_send,
    sib_recv,
    rp_send,
    rp_recv,
    rl_send,
    rl_recv,
    al_send,
    al_recv,
    ap_send,
    ap_recv,
):
    nl, f = feats.shape
    fh = f // 2
    plane, layers = half.shape[1:3]
    me = lax.axis_index("dom")
    chip = me // 2
    core = me % 2
    place = chip % plane
    layer = chip // plane
    sibling = chip * 2 + 1 - core
    blk = 256
    barrier = pltpu.get_barrier_semaphore()

    @pl.loop(1, n)
    def _(k):
        pl.semaphore_signal(
            barrier, inc=1, device_id={"dom": lax.rem(me + k, n)}, device_id_type=MESH
        )

    def a2a_copy(l, k):
        peer = lax.rem(me + k, n)
        return pltpu.make_async_remote_copy(
            src_ref=sb.at[l, peer],
            dst_ref=arr.at[l, me],
            send_sem=a2a_send.at[l, k],
            recv_sem=a2a_recv.at[l, k],
            device_id={"dom": peer},
            device_id_type=MESH,
        )

    def sib_copy(l):
        return pltpu.make_async_remote_copy(
            src_ref=part.at[l, 1 - core],
            dst_ref=sibr.at[l],
            send_sem=sib_send.at[l],
            recv_sem=sib_recv.at[l],
            device_id={"dom": sibling},
            device_id_type=MESH,
        )

    def plane_copy(src, dst, send, recv, l, k):
        to = lax.rem(place + k, plane)
        return pltpu.make_async_remote_copy(
            src_ref=src(to),
            dst_ref=dst,
            send_sem=send.at[l, k],
            recv_sem=recv.at[l, k],
            device_id={"dom": (layer * plane + to) * 2 + core},
            device_id_type=MESH,
        )

    def layer_copy(src, dst, send, recv, l, k):
        to = lax.rem(layer + k, layers)
        return pltpu.make_async_remote_copy(
            src_ref=src(to),
            dst_ref=dst,
            send_sem=send.at[l, k],
            recv_sem=recv.at[l, k],
            device_id={"dom": (to * plane + place) * 2 + core},
            device_id_type=MESH,
        )

    def rs_plane(l, k):
        return plane_copy(
            lambda to: half.at[l, to], rsp.at[l, place], rp_send, rp_recv, l, k
        )

    def rs_layer(l, k):
        return layer_copy(
            lambda to: mid.at[l, to], rsl.at[l, layer], rl_send, rl_recv, l, k
        )

    def ag_layer(l, k):
        own = ag.at[l, core, place, layer]
        return layer_copy(lambda to: own, own, al_send, al_recv, l, k)

    def ag_plane(l, k):
        own = ag.at[l, core, place]
        return plane_copy(lambda to: own, own, ap_send, ap_recv, l, k)

    def fwd_copy(l):
        return pltpu.make_async_remote_copy(
            src_ref=ag.at[l, core],
            dst_ref=ag.at[l, core],
            send_sem=sib_send.at[2 + l],
            recv_sem=sib_recv.at[2 + l],
            device_id={"dom": sibling},
            device_id_type=MESH,
        )

    def each(count, l, copy, action):
        @pl.loop(1, count)
        def _(k):
            getattr(copy(l, k), action)()

    def slot_back(l, g):
        back = mm(rt[0], g[...], 1, 0) + mm(rt[1], g[...], 1, 0)
        left = back[:, :fh].reshape(n, -1, fh)
        right = back[:, fh:].reshape(n, -1, fh)
        sb[l] = jnp.concatenate([left, right], axis=1).astype(BF16)

    def local_part(g, ws):
        @pl.loop(0, nl // blk)
        def _(i):
            rows = pl.ds(pl.multiple_of(i * blk, blk), blk)
            acc_s[rows, :] = mm(dense[0, rows, :], g[...], 1, 0) + mm(
                dense[1, rows, :], g[...], 1, 0
            )
            acc_o[rows, :] = mm(g[rows, :], ws[...], 1, 1)

    def gradient(l, which, h, *terms):
        for i in range(f // blk):
            cols = slice(i * blk, (i + 1) * blk)
            part[l, which, cols, :] = sum(mm(h[:, cols], g[...], 0, 0) for g in terms)

    def finish(l, wn, emit):
        got = arr[l].astype(F32)
        cap = got.shape[1] // 2
        left = got[:, :cap, :].reshape(n * cap, fh).astype(BF16)
        right = got[:, cap:, :].reshape(n * cap, fh).astype(BF16)
        got = jnp.concatenate([left, right], axis=1)

        @pl.loop(0, nl // blk)
        def _(i):
            rows = pl.ds(pl.multiple_of(i * blk, blk), blk)
            summed = acc_s[rows, :] + mm(onehot[rows, :], got, 1, 0)
            high = summed.astype(BF16)
            low[rows, :] = high
            rest[rows, :] = (summed - high.astype(F32)).astype(BF16)
            emit(rows, acc_o[rows, :] + mm(low[rows, :], wn[...], 1, 1))

    def reduce_start(l):
        sib_copy(l).wait_recv()
        mine = part[l, core] + sibr[l]
        half[l] = mine.astype(BF16).reshape(half.shape[1:])
        each(plane, l, rs_plane, "start")

    def reduce_middle(l):
        each(plane, l, rs_plane, "wait_recv")
        total = half[l, place].astype(F32)
        for k in range(1, plane):
            total = total + rsp[l, lax.rem(place + k, plane)].astype(F32)
        mid[l] = total.astype(BF16)
        each(layers, l, rs_layer, "start")

    def reduce_end(l):
        each(layers, l, rs_layer, "wait_recv")
        total = mid[l, layer].astype(F32)
        for k in range(1, layers):
            total = total + rsl[l, lax.rem(layer + k, layers)].astype(F32)
        ag[l, core, place, layer] = total.astype(BF16)
        each(layers, l, ag_layer, "start")

    def spread(l):
        each(layers, l, ag_layer, "wait_recv")
        each(plane, l, ag_plane, "start")

    def forward(l):
        each(plane, l, ag_plane, "wait_recv")
        fwd_copy(l).start()

    slot_back(0, cot)
    arr[0, me] = jnp.zeros_like(arr[0, me])
    arr[1, me] = jnp.zeros_like(arr[1, me])
    pl.semaphore_wait(barrier, n - 1)
    each(n, 0, a2a_copy, "start")
    hid[...] = jnp.maximum(pre[...], jnp.zeros_like(pre))
    local_part(cot, ws2)
    gradient(0, 0, hid, cot)
    onehot[...] = jnp.where(
        lax.broadcasted_iota(jnp.int32, onehot.shape, 0) == idx[...], 1.0, 0.0
    ).astype(BF16)
    each(n, 0, a2a_copy, "wait_recv")

    def emit_two(rows, value):
        up1[rows, :] = jnp.where(pre[rows, :].astype(F32) > 0, value, 0.0).astype(BF16)

    finish(0, wn2, emit_two)
    slot_back(1, up1)
    each(n, 1, a2a_copy, "start")
    gradient(0, 1, hid, low, rest)
    sib_copy(0).start()
    local_part(up1, ws1)
    reduce_start(0)
    gradient(1, 0, feats, up1)
    each(n, 1, a2a_copy, "wait_recv")

    def emit_one(rows, value):
        fg_out[rows, :] = value

    reduce_middle(0)
    finish(1, wn1, emit_one)
    gradient(1, 1, feats, low, rest)
    sib_copy(1).start()
    reduce_end(0)
    reduce_start(1)
    spread(0)
    reduce_middle(1)
    forward(0)
    reduce_end(1)
    spread(1)
    forward(1)
    each(n, 0, a2a_copy, "wait_send")
    each(n, 1, a2a_copy, "wait_send")
    for l in range(2):
        sib_copy(l).wait_send()
        each(plane, l, rs_plane, "wait_send")
        each(layers, l, rs_layer, "wait_send")
        each(layers, l, ag_layer, "wait_send")
        each(plane, l, ag_plane, "wait_send")
    for l, outs in ((0, (gs2_out, gn2_out)), (1, (gs1_out, gn1_out))):
        fwd_copy(l).wait()
        for which, out in enumerate(outs):
            out[...] = ag[l, which].reshape(out.shape)


def per_device(
    feats,
    pre_act,
    cotangent,
    w_self1,
    w_neigh1,
    w_self2,
    w_neigh2,
    local_tiles,
    local_coords,
    remote_tiles,
    remote_rows,
    remote_slots,
    send_rows,
    send_count,
):
    n = lax.axis_size("dom")
    m = n // 2
    nl, f = feats.shape
    cap = send_rows.shape[2]
    slots = n * cap
    vmem = pl.BlockSpec(memory_space=pltpu.VMEM)
    smem = pl.BlockSpec(memory_space=pltpu.SMEM)
    dense, rt = pl.pallas_call(
        dense_kernel,
        out_shape=(
            jax.ShapeDtypeStruct((2, nl, nl), BF16),
            jax.ShapeDtypeStruct((2, slots, nl), BF16),
        ),
        in_specs=[smem, smem, smem, vmem, vmem],
        out_specs=(vmem, vmem),
        scratch_shapes=[pltpu.VMEM((nl, nl), F32), pltpu.VMEM((slots, nl), F32)],
        compiler_params=pltpu.CompilerParams(vmem_limit_bytes=VMEM_LIMIT),
        name="dense",
    )(local_coords, remote_rows, remote_slots, local_tiles, remote_tiles)

    live = jnp.arange(cap)[None, :] < send_count[0][:, None]
    idx = jnp.where(live, send_rows[0], -1).reshape(1, slots)
    plane = 4
    layers = m // plane
    chunk = f // m
    dma = pltpu.SemaphoreType.DMA
    feat_grad, *grads = pl.pallas_call(
        functools.partial(main_kernel, n),
        out_shape=(
            jax.ShapeDtypeStruct((nl, f), F32),
        )
        + (jax.ShapeDtypeStruct((f, f), BF16),) * 4,
        in_specs=[vmem] * 10,
        out_specs=(vmem,) * 5,
        scratch_shapes=[
            pltpu.VMEM((nl, f), BF16),
            pltpu.VMEM((nl, f), BF16),
            pltpu.VMEM((nl, f), BF16),
            pltpu.VMEM((nl, f), BF16),
            pltpu.VMEM((nl, slots), BF16),
            pltpu.VMEM((nl, f), F32),
            pltpu.VMEM((nl, f), F32),
            pltpu.VMEM((2, n, 2 * cap, f // 2), BF16),
            pltpu.VMEM((2, n, 2 * cap, f // 2), BF16),
            pltpu.VMEM((2, 2, f, f), F32),
            pltpu.VMEM((2, f, f), F32),
            pltpu.VMEM((2, plane, layers, chunk, f), BF16),
            pltpu.VMEM((2, plane, layers, chunk, f), BF16),
            pltpu.VMEM((2, layers, chunk, f), BF16),
            pltpu.VMEM((2, layers, chunk, f), BF16),
            pltpu.VMEM((2, 2, plane, layers, chunk, f), BF16),
            dma((2, n)),
            dma((2, n)),
            dma((4,)),
            dma((4,)),
            dma((2, plane)),
            dma((2, plane)),
            dma((2, layers)),
            dma((2, layers)),
            dma((2, layers)),
            dma((2, layers)),
            dma((2, plane)),
            dma((2, plane)),
        ],
        compiler_params=pltpu.CompilerParams(
            collective_id=0, has_side_effects=True, vmem_limit_bytes=VMEM_LIMIT
        ),
        name="main",
    )(
        feats,
        pre_act,
        cotangent,
        w_self1,
        w_neigh1,
        w_self2,
        w_neigh2,
        dense,
        rt,
        idx,
    )
    return (feat_grad, *(grad.astype(F32) for grad in grads))


def solution(mesh):
    return jax.shard_map(
        per_device,
        mesh=mesh,
        in_specs=(
            P(("groups", "dom"), None),
            P(("groups", "dom"), None),
            P(("groups", "dom"), None),
            P(),
            P(),
            P(),
            P(),
            P(("groups", "dom"), None, None),
            P(("groups", "dom"), None),
            P(("groups", "dom"), None, None),
            P(("groups", "dom")),
            P(("groups", "dom")),
            P(("groups", "dom"), None, None),
            P(("groups", "dom"), None),
        ),
        out_specs=(
            P(("groups", "dom"), None),
            P("groups", None),
            P("groups", None),
            P("groups", None),
            P("groups", None),
        ),
        check_vma=False,
    )
```
